32 devices in a mesh: chan: 8 (over z, y), min: 4 (over x, core).
Axes of the slice: x: 2, y: 2, z: 4, core: 2. Of those that a mesh axis runs over, the one named last changes fastest.
Arguments:
- spectra: bfloat16 [2, 32, 128, 2048], P(None, None, 'min', 'chan'), may hold values from -6 to 6
Outputs:
- cross: float32 [2, 32, 2048, 768], P(None, 'min', 'chan')
The draws below stay inside these ranges and needn't reach their ends.
All inputs are finite; a program needn't handle non-finite values.
Results may differ from the reference program's by a relative error of at most 0.0027.
Values may be sent and summed in bfloat16 or wider, within the bound.
A program may use at most 64 MiB of HBM per device.

```python
import jax
import jax.numpy as jnp
from jax import lax

F = 32
CH_DEV = 256
OFFS = 3
CHANNELS = 2048
MINUTES = 128
N_CHAN = 8


def block_scale(stream_key, dims, cuts, least, largest):
    level, own = 1.0, jax.random.fold_in(stream_key, 6)
    for position, shards_of in cuts:
        draws = jnp.exp(jax.random.uniform(jax.random.fold_in(own, position), (shards_of,), jnp.float32, least / len(cuts), largest / len(cuts)))
        level = level * jnp.repeat(draws, dims[position] // shards_of).reshape([-1 if axis == position else 1 for axis in range(len(dims))])
    return level


def noise(rng, shape, scale, most, shards=(), dtype=jnp.bfloat16):
    factor_of = block_scale(rng, shape, shards, -0.22, 0.18) if shards else 1.0
    result = jax.random.normal(rng, shape, jnp.float32) * scale * factor_of
    return jnp.minimum(jnp.maximum(result, -most), most).astype(dtype)


def setup_inputs(seed: int = 0) -> dict:
    key_of = jax.random.split(jax.random.key(seed), 2)
    spectra = noise(key_of[0], (2, F, MINUTES, CHANNELS), 1.0, 6.0, ((2, 4), (3, 8)))
    return dict(spectra=spectra)


water_level = 0.1

def whiten(spectra):
    values = spectra.astype(jnp.float32)
    power = values[0] * values[0] + values[1] * values[1]
    level = lax.optimization_barrier(jnp.mean(power, axis=0, keepdims=True))
    scale = lax.rsqrt(power + water_level * level + 1e-06)
    return (values * scale[None]).astype(jnp.bfloat16)

def reference(spectra):
    white = whiten(spectra)
    blocks = white.reshape(2, F, MINUTES, N_CHAN, CH_DEV)

    def one_bin(freq):
        both = lax.dynamic_index_in_dim(blocks, freq, 1, keepdims=False).astype(jnp.float32)
        left = jnp.concatenate([both[0], both[1]], axis=0)
        real_parts = []
        imag_parts = []
        for shift_k in range(OFFS):
            partner = jnp.roll(both, -shift_k, axis=2)
            right_re = jnp.concatenate([partner[0], partner[1]], axis=0)
            right_im = jnp.concatenate([partner[1], -partner[0]], axis=0)
            real_parts.append(jnp.einsum('mbi,mbj->bij', left, right_re))
            imag_parts.append(jnp.einsum('mbi,mbj->bij', left, right_im))
        real_all = jnp.concatenate(real_parts, axis=-1).reshape(CHANNELS, OFFS * CH_DEV)
        imag_all = jnp.concatenate(imag_parts, axis=-1).reshape(CHANNELS, OFFS * CH_DEV)
        return jnp.stack([real_all, imag_all])
    stacked = lax.map(one_bin, jnp.arange(F))
    return jnp.transpose(stacked, (1, 0, 2, 3)) * MINUTES ** (-0.5)
```

```python
import functools

import jax
import jax.numpy as jnp
from jax import lax
from jax.experimental import pallas as pl
from jax.experimental.pallas import tpu as pltpu
from jax.sharding import PartitionSpec as P

OFFS = 3
AHEAD = 3
LAG = 2

water_level = 0.1

MESH = pl.DeviceIdType.MESH


def exchange_kernel(n_min, n_chan, s_ref, a_ref, white, power, level,
                    x_send, x_recv, z_send, z_recv, y_send, y_recv):
    bins = a_ref.shape[1]
    all_bins = s_ref.shape[1]
    me = lax.axis_index("min")
    block = lax.axis_index("chan")
    odd = lax.rem(block, 2)
    before2 = lax.rem(block + n_chan - 2, n_chan)
    after2 = lax.rem(block + 2, n_chan)
    pair = block + 1 - 2 * odd

    barrier = pltpu.get_barrier_semaphore()
    for r in range(1, n_min):
        pl.semaphore_signal(barrier, inc=1, device_id=(block, lax.rem(me + r, n_min)), device_id_type=MESH)
    for other in (before2, after2, pair):
        pl.semaphore_signal(barrier, inc=1, device_id=(other, me), device_id_type=MESH)

    level[...] = jnp.zeros_like(level)

    def add_power(b, carry):
        re = s_ref[0, b].astype(jnp.float32)
        im = s_ref[1, b].astype(jnp.float32)
        p = re * re + im * im
        power[b] = p
        level[...] += p
        return carry

    lax.fori_loop(0, all_bins, add_power, 0, unroll=8)
    level[...] = level[...] * (water_level / all_bins) + 1e-06

    pl.semaphore_wait(barrier, n_min - 1 + 3)

    def x_copy(f, r):
        return pltpu.make_async_remote_copy(
            src_ref=white.at[f, r - 1], dst_ref=a_ref.at[0, f, me],
            send_sem=x_send.at[f, r - 1], recv_sem=x_recv.at[f, r - 1],
            device_id=(block, lax.rem(me + r, n_min)), device_id_type=MESH)

    def z_copy(f):
        return pltpu.make_async_remote_copy(
            src_ref=a_ref.at[0, f], dst_ref=a_ref.at[2, f],
            send_sem=z_send.at[f], recv_sem=z_recv.at[f],
            device_id=(before2, me), device_id_type=MESH)

    def y_copy(f, slot):
        return pltpu.make_async_remote_copy(
            src_ref=a_ref.at[slot, f], dst_ref=a_ref.at[1, f],
            send_sem=y_send.at[f], recv_sem=y_recv.at[f],
            device_id=(pair, me), device_id_type=MESH)

    def whiten(f):
        for r in list(range(1, n_min)) + [0]:
            b = lax.rem(me + r, n_min) * bins + f
            scale = lax.rsqrt(power[b] + level[...])
            for part in range(2):
                value = (s_ref[part, b].astype(jnp.float32) * scale).astype(jnp.bfloat16)
                if r:
                    white[f, r - 1, part] = value
                else:
                    a_ref[0, f, me, part] = value
            if r:
                x_copy(f, r).start()

    ahead = min(AHEAD, bins)
    lag = min(LAG, bins)

    def first(f, carry):
        whiten(f)
        return carry

    lax.fori_loop(0, ahead, first, 0)

    def step(f, carry):
        @pl.when(f < bins)
        def _():
            for r in range(1, n_min):
                x_copy(f, r).wait_recv()
            z_copy(f).start()

            @pl.when(odd == 1)
            def _():
                y_copy(f, 0).start()

        @pl.when(f + ahead < bins)
        def _():
            whiten(f + ahead)

        @pl.when(f >= lag)
        def _():
            z_copy(f - lag).wait_recv()

            @pl.when(odd == 0)
            def _():
                y_copy(f - lag, 2).start()

        return carry

    lax.fori_loop(0, bins + lag, step, 0)

    def last(f, carry):
        for r in range(1, n_min):
            x_copy(f, r).wait_send()
        z_copy(f).wait_send()
        y_copy(f, 0).wait_send()
        y_copy(f, 0).wait_recv()
        return carry

    lax.fori_loop(0, bins, last, 0)


def exchange(spectra, n_min, n_chan):
    _, all_bins, windows, channels = spectra.shape
    bins = all_bins // n_min
    return pl.pallas_call(
        functools.partial(exchange_kernel, n_min, n_chan),
        out_shape=jax.ShapeDtypeStruct((OFFS, bins, n_min, 2, windows, channels), jnp.bfloat16),
        in_specs=[pl.BlockSpec(memory_space=pltpu.VMEM)],
        out_specs=pl.BlockSpec(memory_space=pltpu.VMEM),
        scratch_shapes=[
            pltpu.VMEM((bins, n_min - 1, 2, windows, channels), jnp.bfloat16),
            pltpu.VMEM((all_bins, windows, channels), jnp.float32),
            pltpu.VMEM((windows, channels), jnp.float32),
            pltpu.SemaphoreType.DMA((bins, n_min - 1)),
            pltpu.SemaphoreType.DMA((bins, n_min - 1)),
            pltpu.SemaphoreType.DMA((bins,)),
            pltpu.SemaphoreType.DMA((bins,)),
            pltpu.SemaphoreType.DMA((bins,)),
            pltpu.SemaphoreType.DMA((bins,)),
        ],
        compiler_params=pltpu.CompilerParams(
            collective_id=0, has_side_effects=True, vmem_limit_bytes=24 * 2 ** 20),
    )(spectra)


def stack_kernel(scale, a_ref, o_ref):
    _, _, n_min, _, windows, channels = a_ref.shape
    depth = n_min * 2 * windows
    own = a_ref[0, 0]
    turned = jnp.concatenate([-own[:, 1:2], own[:, 0:1]], axis=1)
    left = jnp.concatenate(
        [own.reshape(depth, channels), turned.reshape(depth, channels)], axis=1).T
    for k in range(OFFS):
        right = a_ref[k, 0].reshape(depth, channels)
        both = jnp.dot(left, right, preferred_element_type=jnp.float32) * scale
        o_ref[0, 0, :, k * channels:(k + 1) * channels] = both[:channels]
        o_ref[1, 0, :, k * channels:(k + 1) * channels] = both[channels:]


def stack(blocks):
    _, bins, n_min, _, windows, channels = blocks.shape
    return pl.pallas_call(
        functools.partial(stack_kernel, (n_min * windows) ** -0.5),
        out_shape=jax.ShapeDtypeStruct((2, bins, channels, OFFS * channels), jnp.float32),
        grid=(bins,),
        in_specs=[pl.BlockSpec((OFFS, 1, n_min, 2, windows, channels), lambda f: (0, f, 0, 0, 0, 0))],
        out_specs=pl.BlockSpec((2, 1, channels, OFFS * channels), lambda f: (0, f, 0, 0)),
        compiler_params=pltpu.CompilerParams(
            dimension_semantics=("arbitrary",), vmem_limit_bytes=32 * 2 ** 20),
    )(blocks)


def solution(mesh):
    n_min, n_chan = mesh.shape["min"], mesh.shape["chan"]

    def on_device(spectra):
        return stack(exchange(spectra, n_min, n_chan))

    return jax.shard_map(
        on_device,
        mesh=mesh,
        in_specs=(P(None, None, "min", "chan"),),
        out_specs=P(None, "min", "chan", None),
        check_vma=False,
    )
```

```python
import functools

import jax
import jax.numpy as jnp
from jax import lax
from jax.experimental import pallas as pl
from jax.experimental.pallas import tpu as pltpu
from jax.sharding import PartitionSpec as P

OFFS = 3
AHEAD = 3
LAG = 2

water_level = 0.1

MESH = pl.DeviceIdType.MESH


def flipped(index, bits, size):
    result, weight = index, 1
    while weight < size:
        if bits & weight:
            result = result + weight * (1 - 2 * lax.rem(index // weight, 2))
        weight *= 2
    return result


def stacked_kernel(n_min, n_chan, s_ref, o_ref, a_ref, left, white, power, level,
                    x_send, x_recv, z_send, z_recv, y_send, y_recv):
    bins = a_ref.shape[1]
    pairs = n_min // 2
    _, all_bins, windows, channels = s_ref.shape
    depth = n_min * 2 * windows
    norm = (n_min * windows) ** -0.5
    me = lax.axis_index("min")
    block = lax.axis_index("chan")
    odd = lax.rem(block, 2)
    before2 = lax.rem(block + n_chan - 2, n_chan)
    after2 = lax.rem(block + 2, n_chan)
    pair = block + 1 - 2 * odd

    barrier = pltpu.get_barrier_semaphore()
    for r in range(1, n_min):
        pl.semaphore_signal(barrier, inc=1, device_id=(block, flipped(me, r, n_min)), device_id_type=MESH)
    for other in (before2, after2, pair):
        pl.semaphore_signal(barrier, inc=1, device_id=(other, me), device_id_type=MESH)

    level[...] = jnp.zeros_like(level)

    def add_power(b, carry):
        re = s_ref[0, b].astype(jnp.float32)
        im = s_ref[1, b].astype(jnp.float32)
        p = re * re + im * im
        power[b] = p
        level[...] += p
        return carry

    lax.fori_loop(0, all_bins, add_power, 0, unroll=8)
    level[...] = level[...] * (water_level / all_bins) + 1e-06

    pl.semaphore_wait(barrier, n_min - 1 + 3)

    def x_copy(f, r):
        return pltpu.make_async_remote_copy(
            src_ref=white.at[f, r - 1], dst_ref=a_ref.at[0, f, me],
            send_sem=x_send.at[f, r - 1], recv_sem=x_recv.at[f, r - 1],
            device_id=(block, flipped(me, r, n_min)), device_id_type=MESH)

    def of_pair(q):
        return pl.ds(2 * flipped(me // 2, q, pairs), 2)

    def z_copy(f, q):
        return pltpu.make_async_remote_copy(
            src_ref=a_ref.at[0, f, of_pair(q)], dst_ref=a_ref.at[2, f, of_pair(q)],
            send_sem=z_send.at[f, q], recv_sem=z_recv.at[f, q],
            device_id=(before2, me), device_id_type=MESH)

    def y_copy(f, q, slot):
        return pltpu.make_async_remote_copy(
            src_ref=a_ref.at[slot, f, of_pair(q)], dst_ref=a_ref.at[1, f, of_pair(q)],
            send_sem=y_send.at[f, q], recv_sem=y_recv.at[f, q],
            device_id=(pair, me), device_id_type=MESH)

    def whiten(f):
        for r in list(range(2, n_min)) + [1, 0]:
            b = flipped(me, r, n_min) * bins + f
            scale = lax.rsqrt(power[b] + level[...])
            for part in range(2):
                value = (s_ref[part, b].astype(jnp.float32) * scale).astype(jnp.bfloat16)
                if r:
                    white[f, r - 1, part] = value
                else:
                    a_ref[0, f, me, part] = value
            if r:
                x_copy(f, r).start()

    ahead = min(AHEAD, bins)
    lag = min(LAG, bins)

    def first(f, carry):
        whiten(f)
        return carry

    lax.fori_loop(0, ahead, first, 0)

    def pass_on(f, q):
        z_copy(f, q).start()

        @pl.when(odd == 1)
        def _():
            y_copy(f, q, 0).start()

    def turn(f):
        own = a_ref[0, f]
        turned = jnp.concatenate([-own[:, 1:2], own[:, 0:1]], axis=1)
        left[f] = jnp.concatenate(
            [own.reshape(depth, channels), turned.reshape(depth, channels)], axis=1).T

    def multiply(f, k):
        both = jnp.dot(left[f], a_ref[k, f].reshape(depth, channels),
                       preferred_element_type=jnp.float32) * norm
        o_ref[0, f, :, k * channels:(k + 1) * channels] = both[:channels]
        o_ref[1, f, :, k * channels:(k + 1) * channels] = both[channels:]

    def step(f, carry):
        @pl.when(f < bins)
        def _():
            x_copy(f, 1).wait_recv()
            pass_on(f, 0)

        @pl.when(f + ahead < bins)
        def _():
            whiten(f + ahead)

        @pl.when((f >= 1) & (f <= bins))
        def _():
            for q in range(1, pairs):
                x_copy(f - 1, 2 * q).wait_recv()
                x_copy(f - 1, 2 * q + 1).wait_recv()
                pass_on(f - 1, q)
            turn(f - 1)
            multiply(f - 1, 0)

        @pl.when((f >= lag) & (f < bins + lag))
        def _():
            for q in range(pairs):
                z_copy(f - lag, q).wait_recv()

                @pl.when(odd == 0)
                def _():
                    y_copy(f - lag, q, 2).start()

            multiply(f - lag, 2)

        @pl.when(f >= lag + 1)
        def _():
            for q in range(pairs):
                y_copy(f - lag - 1, q, 0).wait_recv()
            multiply(f - lag - 1, 1)

        return carry

    lax.fori_loop(0, bins + lag + 1, step, 0)

    def last(f, carry):
        for r in range(1, n_min):
            x_copy(f, r).wait_send()
        for q in range(pairs):
            z_copy(f, q).wait_send()
            y_copy(f, q, 0).wait_send()
        return carry

    lax.fori_loop(0, bins, last, 0)


def stacked(spectra, n_min, n_chan):
    _, all_bins, windows, channels = spectra.shape
    bins = all_bins // n_min
    return pl.pallas_call(
        functools.partial(stacked_kernel, n_min, n_chan),
        out_shape=jax.ShapeDtypeStruct((2, bins, channels, OFFS * channels), jnp.float32),
        in_specs=[pl.BlockSpec(memory_space=pltpu.VMEM)],
        out_specs=pl.BlockSpec(memory_space=pltpu.VMEM),
        scratch_shapes=[
            pltpu.VMEM((OFFS, bins, n_min, 2, windows, channels), jnp.bfloat16),
            pltpu.VMEM((bins, 2 * channels, n_min * 2 * windows), jnp.bfloat16),
            pltpu.VMEM((bins, n_min - 1, 2, windows, channels), jnp.bfloat16),
            pltpu.VMEM((all_bins, windows, channels), jnp.float32),
            pltpu.VMEM((windows, channels), jnp.float32),
            pltpu.SemaphoreType.DMA((bins, n_min - 1)),
            pltpu.SemaphoreType.DMA((bins, n_min - 1)),
            pltpu.SemaphoreType.DMA((bins, n_min // 2)),
            pltpu.SemaphoreType.DMA((bins, n_min // 2)),
            pltpu.SemaphoreType.DMA((bins, n_min // 2)),
            pltpu.SemaphoreType.DMA((bins, n_min // 2)),
        ],
        compiler_params=pltpu.CompilerParams(
            collective_id=0, has_side_effects=True, vmem_limit_bytes=24 * 2 ** 20),
    )(spectra)


def write_kernel(v_ref, o_ref, sem):
    def copy(part, f):
        return pltpu.make_async_copy(v_ref.at[part, f], o_ref.at[part, f], sem.at[part, f])

    both = [(part, f) for f in range(v_ref.shape[1]) for part in range(2)]
    for at in both:
        copy(*at).start()
    for at in both:
        copy(*at).wait()


def written(result):
    return pl.pallas_call(
        write_kernel,
        out_shape=jax.ShapeDtypeStruct(result.shape, result.dtype),
        in_specs=[pl.BlockSpec(memory_space=pltpu.VMEM)],
        out_specs=pl.BlockSpec(memory_space=pl.ANY),
        scratch_shapes=[pltpu.SemaphoreType.DMA(result.shape[:2])],
        compiler_params=pltpu.CompilerParams(vmem_limit_bytes=24 * 2 ** 20),
    )(result)


def solution(mesh):
    n_min, n_chan = mesh.shape["min"], mesh.shape["chan"]

    def on_device(spectra):
        return written(stacked(spectra, n_min, n_chan))

    return jax.shard_map(
        on_device,
        mesh=mesh,
        in_specs=(P(None, None, "min", "chan"),),
        out_specs=P(None, "min", "chan", None),
        check_vma=False,
    )
```

```python
import functools

import jax
import jax.numpy as jnp
from jax import lax
from jax.experimental import pallas as pl
from jax.experimental.pallas import tpu as pltpu
from jax.sharding import PartitionSpec as P

OFFS = 3
AHEAD = 1
LAG = 2

water_level = 0.1

MESH = pl.DeviceIdType.MESH


def flipped(index, bits, size):
    result, weight = index, 1
    while weight < size:
        if bits & weight:
            result = result + weight * (1 - 2 * lax.rem(index // weight, 2))
        weight *= 2
    return result


def stacked_kernel(n_min, n_chan, s_ref, o_ref, a_ref, left, white, power, level,
                    x_send, x_recv, z_send, z_recv, y_send, y_recv):
    bins = a_ref.shape[1]
    pairs = n_min // 2
    _, all_bins, windows, channels = s_ref.shape
    depth = n_min * 2 * windows
    norm = (n_min * windows) ** -0.5
    me = lax.axis_index("min")
    block = lax.axis_index("chan")
    odd = lax.rem(block, 2)
    before2 = lax.rem(block + n_chan - 2, n_chan)
    after2 = lax.rem(block + 2, n_chan)
    pair = block + 1 - 2 * odd

    barrier = pltpu.get_barrier_semaphore()
    for r in range(1, n_min):
        pl.semaphore_signal(barrier, inc=1, device_id=(block, flipped(me, r, n_min)), device_id_type=MESH)
    for other in (before2, after2, pair):
        pl.semaphore_signal(barrier, inc=1, device_id=(other, me), device_id_type=MESH)

    level[...] = jnp.zeros_like(level)

    def add_power(b, carry):
        re = s_ref[0, b].astype(jnp.float32)
        im = s_ref[1, b].astype(jnp.float32)
        p = re * re + im * im
        power[b] = p
        level[...] += p
        return carry

    lax.fori_loop(0, all_bins, add_power, 0, unroll=8)
    level[...] = level[...] * (water_level / all_bins) + 1e-06

    pl.semaphore_wait(barrier, n_min - 1 + 3)

    def x_copy(f, r):
        return pltpu.make_async_remote_copy(
            src_ref=white.at[f, r - 1], dst_ref=a_ref.at[0, f, me],
            send_sem=x_send.at[f, r - 1], recv_sem=x_recv.at[f, r - 1],
            device_id=(block, flipped(me, r, n_min)), device_id_type=MESH)

    def of_pair(q):
        return pl.ds(2 * flipped(me // 2, q, pairs), 2)

    def z_copy(f, q):
        return pltpu.make_async_remote_copy(
            src_ref=a_ref.at[0, f, of_pair(q)], dst_ref=a_ref.at[2, f, of_pair(q)],
            send_sem=z_send.at[f, q], recv_sem=z_recv.at[f, q],
            device_id=(before2, me), device_id_type=MESH)

    def y_copy(f, q, slot):
        return pltpu.make_async_remote_copy(
            src_ref=a_ref.at[slot, f, of_pair(q)], dst_ref=a_ref.at[1, f, of_pair(q)],
            send_sem=y_send.at[f, q], recv_sem=y_recv.at[f, q],
            device_id=(pair, me), device_id_type=MESH)

    def whiten(f):
        for r in list(range(2, n_min)) + [1, 0]:
            b = flipped(me, r, n_min) * bins + f
            scale = lax.rsqrt(power[b] + level[...])
            for part in range(2):
                value = (s_ref[part, b].astype(jnp.float32) * scale).astype(jnp.bfloat16)
                if r:
                    white[f, r - 1, part] = value
                else:
                    a_ref[0, f, me, part] = value
            if r:
                x_copy(f, r).start()

    ahead = min(AHEAD, bins)
    lag = min(LAG, bins)

    def first(f, carry):
        whiten(f)
        return carry

    lax.fori_loop(0, ahead, first, 0)

    def pass_on(f, q):
        z_copy(f, q).start()

        @pl.when(odd == 1)
        def _():
            y_copy(f, q, 0).start()

    def turn(f):
        own = a_ref[0, f]
        turned = jnp.concatenate([-own[:, 1:2], own[:, 0:1]], axis=1)
        left[f] = jnp.concatenate(
            [own.reshape(depth, channels), turned.reshape(depth, channels)], axis=1).T

    def multiply(f, k):
        both = jnp.dot(left[f], a_ref[k, f].reshape(depth, channels),
                       preferred_element_type=jnp.float32) * norm
        o_ref[0, f, :, k * channels:(k + 1) * channels] = both[:channels]
        o_ref[1, f, :, k * channels:(k + 1) * channels] = both[channels:]

    def forward(f, q):
        z_copy(f, q).wait_recv()

        @pl.when(odd == 0)
        def _():
            y_copy(f, q, 2).start()

    def step(f, carry):
        @pl.when(f < bins)
        def _():
            x_copy(f, 1).wait_recv()
            pass_on(f, 0)

        @pl.when(f + ahead < bins)
        def _():
            whiten(f + ahead)

        @pl.when((f >= 1) & (f <= bins))
        def _():
            for q in range(1, pairs):
                x_copy(f - 1, 2 * q).wait_recv()
                x_copy(f - 1, 2 * q + 1).wait_recv()
                pass_on(f - 1, q)
            forward(f - 1, 0)
            turn(f - 1)
            multiply(f - 1, 0)

        @pl.when((f >= lag) & (f < bins + lag))
        def _():
            for q in range(1, pairs):
                forward(f - lag, q)
            multiply(f - lag, 2)

        @pl.when(f >= lag + 1)
        def _():
            for q in range(pairs):
                y_copy(f - lag - 1, q, 0).wait_recv()
            multiply(f - lag - 1, 1)

        return carry

    lax.fori_loop(0, bins + lag + 1, step, 0)

    def last(f, carry):
        for r in range(1, n_min):
            x_copy(f, r).wait_send()
        for q in range(pairs):
            z_copy(f, q).wait_send()
            y_copy(f, q, 0).wait_send()
        return carry

    lax.fori_loop(0, bins, last, 0)


def stacked(spectra, n_min, n_chan):
    _, all_bins, windows, channels = spectra.shape
    bins = all_bins // n_min
    return pl.pallas_call(
        functools.partial(stacked_kernel, n_min, n_chan),
        out_shape=jax.ShapeDtypeStruct((2, bins, channels, OFFS * channels), jnp.float32),
        in_specs=[pl.BlockSpec(memory_space=pltpu.VMEM)],
        out_specs=pl.BlockSpec(memory_space=pltpu.VMEM),
        scratch_shapes=[
            pltpu.VMEM((OFFS, bins, n_min, 2, windows, channels), jnp.bfloat16),
            pltpu.VMEM((bins, 2 * channels, n_min * 2 * windows), jnp.bfloat16),
            pltpu.VMEM((bins, n_min - 1, 2, windows, channels), jnp.bfloat16),
            pltpu.VMEM((all_bins, windows, channels), jnp.float32),
            pltpu.VMEM((windows, channels), jnp.float32),
            pltpu.SemaphoreType.DMA((bins, n_min - 1)),
            pltpu.SemaphoreType.DMA((bins, n_min - 1)),
            pltpu.SemaphoreType.DMA((bins, n_min // 2)),
            pltpu.SemaphoreType.DMA((bins, n_min // 2)),
            pltpu.SemaphoreType.DMA((bins, n_min // 2)),
            pltpu.SemaphoreType.DMA((bins, n_min // 2)),
        ],
        compiler_params=pltpu.CompilerParams(
            collective_id=0, has_side_effects=True, vmem_limit_bytes=24 * 2 ** 20),
    )(spectra)


def write_kernel(v_ref, o_ref, sem):
    def copy(part, f):
        return pltpu.make_async_copy(v_ref.at[part, f], o_ref.at[part, f], sem.at[part, f])

    both = [(part, f) for f in range(v_ref.shape[1]) for part in range(2)]
    for at in both:
        copy(*at).start()
    for at in both:
        copy(*at).wait()


def written(result):
    return pl.pallas_call(
        write_kernel,
        out_shape=jax.ShapeDtypeStruct(result.shape, result.dtype),
        in_specs=[pl.BlockSpec(memory_space=pltpu.VMEM)],
        out_specs=pl.BlockSpec(memory_space=pl.ANY),
        scratch_shapes=[pltpu.SemaphoreType.DMA(result.shape[:2])],
        compiler_params=pltpu.CompilerParams(vmem_limit_bytes=24 * 2 ** 20),
    )(result)


def solution(mesh):
    n_min, n_chan = mesh.shape["min"], mesh.shape["chan"]

    def on_device(spectra):
        return written(stacked(spectra, n_min, n_chan))

    return jax.shard_map(
        on_device,
        mesh=mesh,
        in_specs=(P(None, None, "min", "chan"),),
        out_specs=P(None, "min", "chan", None),
        check_vma=False,
    )
```

```python
import functools

import jax
import jax.numpy as jnp
from jax import lax
from jax.experimental import pallas as pl
from jax.experimental.pallas import tpu as pltpu
from jax.sharding import PartitionSpec as P

OFFS = 3
AHEAD = 1
LAG = 2

water_level = 0.1

MESH = pl.DeviceIdType.MESH


def flipped(index, bits, size):
    result, weight = index, 1
    while weight < size:
        if bits & weight:
            result = result + weight * (1 - 2 * lax.rem(index // weight, 2))
        weight *= 2
    return result


def stacked_kernel(n_min, n_chan, s_ref, o_ref, a_ref, left, white, power, level,
                    x_send, x_recv, z_send, z_recv, y_send, y_recv):
    bins = a_ref.shape[1]
    pairs = n_min // 2
    _, all_bins, windows, channels = s_ref.shape
    depth = n_min * 2 * windows
    norm = (n_min * windows) ** -0.5
    me = lax.axis_index("min")
    block = lax.axis_index("chan")
    odd = lax.rem(block, 2)
    before2 = lax.rem(block + n_chan - 2, n_chan)
    after2 = lax.rem(block + 2, n_chan)
    pair = block + 1 - 2 * odd

    barrier = pltpu.get_barrier_semaphore()
    for r in range(1, n_min):
        pl.semaphore_signal(barrier, inc=1, device_id=(block, flipped(me, r, n_min)), device_id_type=MESH)
    for other in (before2, after2, pair):
        pl.semaphore_signal(barrier, inc=1, device_id=(other, me), device_id_type=MESH)

    def add_power(b, carry):
        re = s_ref[0, b].astype(jnp.float32)
        im = s_ref[1, b].astype(jnp.float32)
        p = re * re + im * im
        power[b] = p
        return carry + p

    total = lax.fori_loop(0, all_bins, add_power, jnp.zeros(level.shape, jnp.float32), unroll=8)
    level[...] = total * (water_level / all_bins) + 1e-06

    pl.semaphore_wait(barrier, n_min - 1 + 3)

    def x_copy(f, r):
        return pltpu.make_async_remote_copy(
            src_ref=white.at[f, r - 1], dst_ref=a_ref.at[0, f, me],
            send_sem=x_send.at[f, r - 1], recv_sem=x_recv.at[f, r - 1],
            device_id=(block, flipped(me, r, n_min)), device_id_type=MESH)

    def of_pair(q):
        return pl.ds(2 * flipped(me // 2, q, pairs), 2)

    def z_copy(f, q):
        return pltpu.make_async_remote_copy(
            src_ref=a_ref.at[0, f, of_pair(q)], dst_ref=a_ref.at[2, f, of_pair(q)],
            send_sem=z_send.at[f, q], recv_sem=z_recv.at[f, q],
            device_id=(before2, me), device_id_type=MESH)

    def y_copy(f, q, slot):
        return pltpu.make_async_remote_copy(
            src_ref=a_ref.at[slot, f, of_pair(q)], dst_ref=a_ref.at[1, f, of_pair(q)],
            send_sem=y_send.at[f, q], recv_sem=y_recv.at[f, q],
            device_id=(pair, me), device_id_type=MESH)

    def whiten(f):
        for r in [1, 0] + list(range(2, n_min)):
            b = flipped(me, r, n_min) * bins + f
            scale = lax.rsqrt(power[b] + level[...])
            for part in range(2):
                value = (s_ref[part, b].astype(jnp.float32) * scale).astype(jnp.bfloat16)
                if r:
                    white[f, r - 1, part] = value
                else:
                    a_ref[0, f, me, part] = value
            if r:
                x_copy(f, r).start()

    ahead = min(AHEAD, bins)
    lag = min(LAG, bins)

    def first(f, carry):
        whiten(f)
        return carry

    lax.fori_loop(0, ahead, first, 0)

    def pass_on(f, q):
        z_copy(f, q).start()

        @pl.when(odd == 1)
        def _():
            y_copy(f, q, 0).start()

    def turn(f):
        own = a_ref[0, f]
        turned = jnp.concatenate([-own[:, 1:2], own[:, 0:1]], axis=1)
        left[f] = jnp.concatenate(
            [own.reshape(depth, channels), turned.reshape(depth, channels)], axis=1).T

    def multiply(f, k):
        both = jnp.dot(left[f], a_ref[k, f].reshape(depth, channels),
                       preferred_element_type=jnp.float32) * norm
        o_ref[0, f, :, k * channels:(k + 1) * channels] = both[:channels]
        o_ref[1, f, :, k * channels:(k + 1) * channels] = both[channels:]

    def forward(f, q):
        z_copy(f, q).wait_recv()

        @pl.when(odd == 0)
        def _():
            y_copy(f, q, 2).start()

    def step(f, carry):
        @pl.when(f < bins)
        def _():
            x_copy(f, 1).wait_recv()
            pass_on(f, 0)

        @pl.when(f + ahead < bins)
        def _():
            whiten(f + ahead)

        @pl.when((f >= 1) & (f <= bins))
        def _():
            for q in range(1, pairs):
                x_copy(f - 1, 2 * q).wait_recv()
                x_copy(f - 1, 2 * q + 1).wait_recv()
                pass_on(f - 1, q)
            forward(f - 1, 0)
            turn(f - 1)
            multiply(f - 1, 0)

        @pl.when((f >= lag) & (f < bins + lag))
        def _():
            for q in range(1, pairs):
                forward(f - lag, q)
            multiply(f - lag, 2)

        @pl.when(f >= lag + 1)
        def _():
            for q in range(pairs):
                y_copy(f - lag - 1, q, 0).wait_recv()
            multiply(f - lag - 1, 1)

        return carry

    lax.fori_loop(0, bins + lag + 1, step, 0)

    def last(f, carry):
        for r in range(1, n_min):
            x_copy(f, r).wait_send()
        for q in range(pairs):
            z_copy(f, q).wait_send()
            y_copy(f, q, 0).wait_send()
        return carry

    lax.fori_loop(0, bins, last, 0)


def stacked(spectra, n_min, n_chan):
    _, all_bins, windows, channels = spectra.shape
    bins = all_bins // n_min
    return pl.pallas_call(
        functools.partial(stacked_kernel, n_min, n_chan),
        out_shape=jax.ShapeDtypeStruct((2, bins, channels, OFFS * channels), jnp.float32),
        in_specs=[pl.BlockSpec(memory_space=pltpu.VMEM)],
        out_specs=pl.BlockSpec(memory_space=pltpu.VMEM),
        scratch_shapes=[
            pltpu.VMEM((OFFS, bins, n_min, 2, windows, channels), jnp.bfloat16),
            pltpu.VMEM((bins, 2 * channels, n_min * 2 * windows), jnp.bfloat16),
            pltpu.VMEM((bins, n_min - 1, 2, windows, channels), jnp.bfloat16),
            pltpu.VMEM((all_bins, windows, channels), jnp.float32),
            pltpu.VMEM((windows, channels), jnp.float32),
            pltpu.SemaphoreType.DMA((bins, n_min - 1)),
            pltpu.SemaphoreType.DMA((bins, n_min - 1)),
            pltpu.SemaphoreType.DMA((bins, n_min // 2)),
            pltpu.SemaphoreType.DMA((bins, n_min // 2)),
            pltpu.SemaphoreType.DMA((bins, n_min // 2)),
            pltpu.SemaphoreType.DMA((bins, n_min // 2)),
        ],
        compiler_params=pltpu.CompilerParams(
            collective_id=0, has_side_effects=True, vmem_limit_bytes=24 * 2 ** 20),
    )(spectra)


def write_kernel(v_ref, o_ref, sem):
    def copy(part, f):
        return pltpu.make_async_copy(v_ref.at[part, f], o_ref.at[part, f], sem.at[part, f])

    both = [(part, f) for f in range(v_ref.shape[1]) for part in range(2)]
    for at in both:
        copy(*at).start()
    for at in both:
        copy(*at).wait()


def written(result):
    return pl.pallas_call(
        write_kernel,
        out_shape=jax.ShapeDtypeStruct(result.shape, result.dtype),
        in_specs=[pl.BlockSpec(memory_space=pltpu.VMEM)],
        out_specs=pl.BlockSpec(memory_space=pl.ANY),
        scratch_shapes=[pltpu.SemaphoreType.DMA(result.shape[:2])],
        compiler_params=pltpu.CompilerParams(vmem_limit_bytes=24 * 2 ** 20),
    )(result)


def solution(mesh):
    n_min, n_chan = mesh.shape["min"], mesh.shape["chan"]

    def on_device(spectra):
        return written(stacked(spectra, n_min, n_chan))

    return jax.shard_map(
        on_device,
        mesh=mesh,
        in_specs=(P(None, None, "min", "chan"),),
        out_specs=P(None, "min", "chan", None),
        check_vma=False,
    )
```

```python
import functools

import jax
import jax.numpy as jnp
from jax import lax
from jax.experimental import pallas as pl
from jax.experimental.pallas import tpu as pltpu
from jax.sharding import PartitionSpec as P

OFFS = 3
AHEAD = 1
LAG = 2

water_level = 0.1

MESH = pl.DeviceIdType.MESH


def flipped(index, bits, size):
    result, weight = index, 1
    while weight < size:
        if bits & weight:
            result = result + weight * (1 - 2 * lax.rem(index // weight, 2))
        weight *= 2
    return result


def stacked_kernel(n_min, n_chan, s_ref, o_ref, a_ref, left, white, power, level,
                    x_send, x_recv, z_send, z_recv, y_send, y_recv):
    bins = a_ref.shape[1]
    pairs = n_min // 2
    _, all_bins, windows, channels = s_ref.shape
    depth = n_min * 2 * windows
    norm = (n_min * windows) ** -0.5
    me = lax.axis_index("min")
    block = lax.axis_index("chan")
    odd = lax.rem(block, 2)
    before2 = lax.rem(block + n_chan - 2, n_chan)
    after2 = lax.rem(block + 2, n_chan)
    pair = block + 1 - 2 * odd

    barrier = pltpu.get_barrier_semaphore()
    for r in range(1, n_min):
        pl.semaphore_signal(barrier, inc=1, device_id=(block, flipped(me, r, n_min)), device_id_type=MESH)
    for other in (before2, after2, pair):
        pl.semaphore_signal(barrier, inc=1, device_id=(other, me), device_id_type=MESH)

    level[...] = jnp.zeros_like(level)

    def add_power(b, carry):
        re = s_ref[0, b].astype(jnp.float32)
        im = s_ref[1, b].astype(jnp.float32)
        p = re * re + im * im
        power[b] = p
        level[...] += p
        return carry

    lax.fori_loop(0, all_bins, add_power, 0, unroll=8)
    level[...] = level[...] * (water_level / all_bins) + 1e-06

    pl.semaphore_wait(barrier, n_min - 1 + 3)

    def x_copy(f, r):
        return pltpu.make_async_remote_copy(
            src_ref=white.at[f, r - 1], dst_ref=a_ref.at[0, f, me],
            send_sem=x_send.at[f, r - 1], recv_sem=x_recv.at[f, r - 1],
            device_id=(block, flipped(me, r, n_min)), device_id_type=MESH)

    def of_pair(q):
        return pl.ds(2 * flipped(me // 2, q, pairs), 2)

    def z_copy(f, q):
        return pltpu.make_async_remote_copy(
            src_ref=a_ref.at[0, f, of_pair(q)], dst_ref=a_ref.at[2, f, of_pair(q)],
            send_sem=z_send.at[f, q], recv_sem=z_recv.at[f, q],
            device_id=(before2, me), device_id_type=MESH)

    def y_copy(f, q, slot):
        return pltpu.make_async_remote_copy(
            src_ref=a_ref.at[slot, f, of_pair(q)], dst_ref=a_ref.at[1, f, of_pair(q)],
            send_sem=y_send.at[f, q], recv_sem=y_recv.at[f, q],
            device_id=(pair, me), device_id_type=MESH)

    def whiten(f):
        for r in list(range(2, n_min)) + [1, 0]:
            b = flipped(me, r, n_min) * bins + f
            scale = lax.rsqrt(power[b] + level[...])
            for part in range(2):
                value = (s_ref[part, b].astype(jnp.float32) * scale).astype(jnp.bfloat16)
                if r:
                    white[f, r - 1, part] = value
                else:
                    a_ref[0, f, me, part] = value
            if r:
                x_copy(f, r).start()

    ahead = min(AHEAD, bins)
    lag = min(LAG, bins)

    def first(f, carry):
        whiten(f)
        return carry

    lax.fori_loop(0, ahead, first, 0)

    def pass_on(f, q):
        z_copy(f, q).start()

        @pl.when(odd == 1)
        def _():
            y_copy(f, q, 0).start()

    def turn(f):
        own = a_ref[0, f]
        turned = jnp.concatenate([-own[:, 1:2], own[:, 0:1]], axis=1)
        left[f] = jnp.concatenate(
            [own.reshape(depth, channels), turned.reshape(depth, channels)], axis=1).T

    def multiply(f, k):
        both = jnp.dot(left[f], a_ref[k, f].reshape(depth, channels),
                       preferred_element_type=jnp.float32) * norm
        o_ref[0, f, :, k * channels:(k + 1) * channels] = both[:channels]
        o_ref[1, f, :, k * channels:(k + 1) * channels] = both[channels:]

    def forward(f, q):
        z_copy(f, q).wait_recv()

        @pl.when(odd == 0)
        def _():
            y_copy(f, q, 2).start()

    def step(f, carry):
        @pl.when(f < bins)
        def _():
            x_copy(f, 1).wait_recv()
            pass_on(f, 0)

        @pl.when((f >= 1) & (f <= bins))
        def _():
            for q in range(1, pairs):
                x_copy(f - 1, 2 * q).wait_recv()
                x_copy(f - 1, 2 * q + 1).wait_recv()
                pass_on(f - 1, q)

        @pl.when(f + ahead < bins)
        def _():
            whiten(f + ahead)

        @pl.when((f >= 1) & (f <= bins))
        def _():
            forward(f - 1, 0)

        @pl.when((f >= lag) & (f < bins + lag))
        def _():
            for q in range(1, pairs):
                forward(f - lag, q)

        @pl.when((f >= 1) & (f <= bins))
        def _():
            turn(f - 1)
            multiply(f - 1, 0)

        @pl.when((f >= lag) & (f < bins + lag))
        def _():
            multiply(f - lag, 2)

        @pl.when(f >= lag + 1)
        def _():
            for q in range(pairs):
                y_copy(f - lag - 1, q, 0).wait_recv()
            multiply(f - lag - 1, 1)


        return carry

    lax.fori_loop(0, bins + lag + 1, step, 0)

    def last(f, carry):
        for r in range(1, n_min):
            x_copy(f, r).wait_send()
        for q in range(pairs):
            z_copy(f, q).wait_send()
            y_copy(f, q, 0).wait_send()
        return carry

    lax.fori_loop(0, bins, last, 0)


def stacked(spectra, n_min, n_chan):
    _, all_bins, windows, channels = spectra.shape
    bins = all_bins // n_min
    return pl.pallas_call(
        functools.partial(stacked_kernel, n_min, n_chan),
        out_shape=jax.ShapeDtypeStruct((2, bins, channels, OFFS * channels), jnp.float32),
        in_specs=[pl.BlockSpec(memory_space=pltpu.VMEM)],
        out_specs=pl.BlockSpec(memory_space=pltpu.VMEM),
        scratch_shapes=[
            pltpu.VMEM((OFFS, bins, n_min, 2, windows, channels), jnp.bfloat16),
            pltpu.VMEM((bins, 2 * channels, n_min * 2 * windows), jnp.bfloat16),
            pltpu.VMEM((bins, n_min - 1, 2, windows, channels), jnp.bfloat16),
            pltpu.VMEM((all_bins, windows, channels), jnp.float32),
            pltpu.VMEM((windows, channels), jnp.float32),
            pltpu.SemaphoreType.DMA((bins, n_min - 1)),
            pltpu.SemaphoreType.DMA((bins, n_min - 1)),
            pltpu.SemaphoreType.DMA((bins, n_min // 2)),
            pltpu.SemaphoreType.DMA((bins, n_min // 2)),
            pltpu.SemaphoreType.DMA((bins, n_min // 2)),
            pltpu.SemaphoreType.DMA((bins, n_min // 2)),
        ],
        compiler_params=pltpu.CompilerParams(
            collective_id=0, has_side_effects=True, vmem_limit_bytes=24 * 2 ** 20),
    )(spectra)


def write_kernel(v_ref, o_ref, sem):
    def copy(part, f):
        return pltpu.make_async_copy(v_ref.at[part, f], o_ref.at[part, f], sem.at[part, f])

    both = [(part, f) for f in range(v_ref.shape[1]) for part in range(2)]
    for at in both:
        copy(*at).start()
    for at in both:
        copy(*at).wait()


def written(result):
    return pl.pallas_call(
        write_kernel,
        out_shape=jax.ShapeDtypeStruct(result.shape, result.dtype),
        in_specs=[pl.BlockSpec(memory_space=pltpu.VMEM)],
        out_specs=pl.BlockSpec(memory_space=pl.ANY),
        scratch_shapes=[pltpu.SemaphoreType.DMA(result.shape[:2])],
        compiler_params=pltpu.CompilerParams(vmem_limit_bytes=24 * 2 ** 20),
    )(result)


def solution(mesh):
    n_min, n_chan = mesh.shape["min"], mesh.shape["chan"]

    def on_device(spectra):
        return written(stacked(spectra, n_min, n_chan))

    return jax.shard_map(
        on_device,
        mesh=mesh,
        in_specs=(P(None, None, "min", "chan"),),
        out_specs=P(None, "min", "chan", None),
        check_vma=False,
    )
```
